256 devices in a mesh: dp: 16 (over z, core), tensor: 16 (over x, y).
Axes of the slice: x: 4, y: 4, z: 8, core: 2. Of those that a mesh axis runs over, the one named last changes fastest.
Arguments:
- attn_out: bfloat16 [12288, 8192], P('dp', 'tensor'), may hold values from -0.21875 to 0.21875
- grad_out: bfloat16 [12288, 4096], P(('dp', 'tensor')), may hold values from -6 to 6
- weight: bfloat16 [8192, 4096], P('tensor'), may hold values from -0.09375 to 0.09375
- error_feed: bfloat16 [131072, 4096], P(('dp', 'tensor')), may hold values from -6 to 6
- warm_basis: float32 [4096, 64], replicated, may hold values from -0.09375 to 0.09375
Outputs:
- grad_in: bfloat16 [12288, 8192], P('dp', 'tensor')
- new_error: bfloat16 [131072, 4096], P(('dp', 'tensor'))
- new_basis: float32 [4096, 64], replicated
The draws below stay inside these ranges and needn't reach their ends.
All inputs are finite; a program needn't handle non-finite values.
Results may differ from the reference program's by a relative error of at most 0.013.
Values may be sent and summed in bfloat16 or wider, within the bound.
No kernel may reach another device: no remote copies, remote signals or barrier semaphores. Data moves between devices by JAX's collectives and lax.ppermute only.
A program may use at most 128 MiB of HBM per device.

```python
import jax
import jax.numpy as jnp
from jax import lax

D = 4096
HD = 8192
RANK = 64
TOK = 768
N_DP = 16


def shard_levels(rng, shape, pieces, low, top_value):
    level = 1.0
    for position, parts in pieces:
        draws = jax.random.uniform(jax.random.fold_in(jax.random.fold_in(rng, 6), position), (parts,), jnp.float32, low / len(pieces), top_value / len(pieces))
        level = level * jnp.repeat(jnp.exp(draws), shape[position] // parts).reshape((-1,) + (1,) * (len(shape) - 1 - position))
    return level


def normal_values(rng, extent, deviation, bound, split=(), held_as=jnp.bfloat16):
    level = shard_levels(rng, extent, split, -0.22, 0.18) if split else 1.0
    result = jax.random.normal(rng, extent, jnp.float32) * deviation * level
    return jnp.minimum(jnp.maximum(result, -bound), bound).astype(held_as)


def setup_inputs(seed: int = 0) -> dict:
    keys = jax.random.split(jax.random.key(seed), 6)
    attn_out = normal_values(keys[0], (TOK * N_DP, HD), TOK ** -0.5, 0.21875, ((0, 16), (1, 16)))
    grad_out = normal_values(keys[1], (TOK * N_DP, D), 1.0, 6.0, ((0, 256),))
    weight = normal_values(keys[2], (HD, D), D ** -0.5, 0.09375, ((0, 16),))
    error_feed = normal_values(keys[3], (N_DP * HD, D), 1.0, 6.0, ((0, 256),))
    warm_basis = normal_values(keys[4], (D, RANK), D ** -0.5, 0.09375, (), jnp.float32)
    return {"attn_out": attn_out, "grad_out": grad_out, "weight": weight, "error_feed": error_feed, "warm_basis": warm_basis}


def reference(attn_out, grad_out, weight, error_feed, warm_basis):
    high = lax.Precision.HIGHEST
    merged_list = []
    grad_list = []
    panel = jnp.zeros((HD, RANK), jnp.float32)
    for replica in range(N_DP):
        act_rows = attn_out[replica * TOK:(replica + 1) * TOK]
        cot_rows = grad_out[replica * TOK:(replica + 1) * TOK]
        gradient = jnp.dot(act_rows.T.astype(jnp.float32), cot_rows.astype(jnp.float32), preferred_element_type=jnp.float32)
        grad_list.append(jnp.dot(cot_rows.astype(jnp.float32), weight.T.astype(jnp.float32), preferred_element_type=jnp.float32).astype(jnp.bfloat16))
        merged = gradient + error_feed[replica * HD:(replica + 1) * HD].astype(jnp.float32)
        merged_list.append(merged)
        panel = panel + jnp.dot(merged, warm_basis, precision=high)
    panel = panel / N_DP
    gram_matrix = jnp.dot(panel.T, panel, precision=high)
    factor = jnp.linalg.cholesky(gram_matrix)
    ortho = lax.linalg.triangular_solve(factor, panel, left_side=False, lower=True, transpose_a=True)
    new_basis = jnp.zeros((D, RANK), jnp.float32)
    for replica in range(N_DP):
        new_basis = new_basis + jnp.dot(merged_list[replica].T, ortho, precision=high)
    new_basis = new_basis / N_DP
    approx = jnp.dot(ortho, new_basis.T, precision=high)
    new_error = jnp.concatenate([(m - approx).astype(jnp.bfloat16) for m in merged_list], axis=0)
    grad_in = jnp.concatenate(grad_list, axis=0)
    return (grad_in, new_error, new_basis)
```

```python
import jax
import jax.numpy as jnp
from jax import lax
from jax.sharding import PartitionSpec as P

F32 = jnp.float32
BF16 = jnp.bfloat16


def split_high_low(value):
    high = value.astype(BF16)
    return high, (value - high.astype(F32)).astype(BF16)


def dot(a, b, ca, cb):
    return lax.dot_general(a, b, (((ca,), (cb,)), ((), ())), preferred_element_type=F32)


def inverse_factor(gram):
    factor = jnp.linalg.cholesky(gram)
    eye = jnp.eye(gram.shape[0], dtype=F32)
    return lax.linalg.triangular_solve(factor, eye, left_side=True, lower=True)


def shards(attn, cot, weight, error, warm):
    high = lax.Precision.HIGHEST
    dp = lax.axis_size("dp")
    group = lax.axis_size("tensor")
    zs = dp // 2
    core = lax.axis_index("dp") % 2
    rank = warm.shape[1]
    feats = attn.shape[1]
    width = cot.shape[1]
    tok = cot.shape[0]
    pair = [(i, i ^ 1) for i in range(dp)]
    z_groups = [list(range(c, dp, 2)) for c in range(2)]

    def swap(value):
        return lax.ppermute(value, "dp", pair)

    def exchange(value, axis, groups=None):
        return lax.all_to_all(value, axis, 0, 0, tiled=True, axis_index_groups=groups)

    def both_halves(mine):
        other = swap(mine)
        first = jnp.where(core == 0, mine, other)
        second = jnp.where(core == 0, other, mine)
        return first, second

    cot_all = lax.all_gather(cot, "tensor", axis=0, tiled=True)

    warm_2 = jnp.concatenate(split_high_low(warm), axis=1)
    q_2 = dot(cot, warm_2, 1, 0)
    q_2 = jnp.concatenate(split_high_low(q_2[:, :rank] + q_2[:, rank:]), axis=1)
    q_all = exchange(jnp.tile(q_2, (group, 1)), "tensor")
    e_2 = dot(warm_2, error, 0, 1)
    p_2 = dot(q_all, attn, 0, 0) + e_2
    part = p_2[:rank] + p_2[rank:]
    half = feats // 2
    mine = lax.dynamic_slice_in_dim(part, core * half, half, 1)
    other = lax.dynamic_slice_in_dim(part, (1 - core) * half, half, 1)
    mine = (mine + swap(other)).astype(BF16)
    mine = exchange(jnp.broadcast_to(mine[None], (zs, rank, half)), "dp", z_groups)
    mine = jnp.sum(mine.astype(F32), axis=0) / dp
    panel = jnp.concatenate(both_halves(mine), axis=1)

    panel_2 = jnp.concatenate(split_high_low(panel), axis=0)
    s_2 = dot(attn, panel_2, 1, 1)
    s_2 = jnp.concatenate(split_high_low(s_2[:, :rank] + s_2[:, rank:]), axis=1)
    gram = lax.dot_general(panel, panel, (((1,), (1,)), ((), ())), precision=high)
    gram = jnp.concatenate(split_high_low(gram), axis=1)
    pack = jnp.concatenate(
        [s_2.reshape(group, tok, 2 * rank), jnp.broadcast_to(gram[None], (group, rank, 2 * rank))], axis=1
    )
    pack = jnp.sum(exchange(pack, "tensor").astype(F32), axis=0)
    pack = pack[:, :rank] + pack[:, rank:]
    s_loc, gram = pack[:tok], pack[tok:]
    inverse = inverse_factor(gram)

    s_loc_2 = jnp.concatenate(split_high_low(s_loc), axis=1)
    b_2 = dot(s_loc_2, cot, 0, 0) + dot(panel_2, error, 1, 0)
    basis = b_2[:rank] + b_2[rank:]
    half = width // 2
    mine = lax.dynamic_slice_in_dim(basis, core * half, half, 1)
    other = lax.dynamic_slice_in_dim(basis, (1 - core) * half, half, 1)
    mine = (mine + swap(other)).astype(BF16)
    piece = half // group
    mine = mine.reshape(rank, group, piece).transpose(1, 0, 2)
    mine = jnp.sum(exchange(mine, "tensor").astype(F32), axis=0).astype(BF16)
    mine = exchange(jnp.broadcast_to(mine[None], (zs, rank, piece)), "dp", z_groups)
    mine = jnp.sum(mine.astype(F32), axis=0) / dp
    mine = jnp.dot(inverse, mine, precision=high).astype(BF16)
    mine = exchange(jnp.broadcast_to(mine[None], (group, rank, piece)), "tensor")
    first, second = both_halves(mine)
    basis = jnp.concatenate([first, second], axis=0).transpose(1, 0, 2).reshape(rank, width)
    new_basis = basis.T.astype(F32)

    grad_in = dot(cot_all, weight, 1, 1).astype(BF16)
    merged = dot(attn, cot_all, 0, 0) + error.astype(F32)
    ortho = jnp.dot(inverse, panel, precision=high)
    ortho_2 = jnp.concatenate(split_high_low(ortho), axis=0)
    approx = dot(ortho_2, jnp.concatenate([basis, basis], axis=0), 0, 0)
    new_error = (merged - approx).astype(BF16)
    return grad_in, new_error, new_basis


def solution(mesh):
    in_specs = (
        P("dp", "tensor"),
        P(("dp", "tensor"), None),
        P("tensor", None),
        P(("dp", "tensor"), None),
        P(),
    )
    out_specs = (P("dp", "tensor"), P(("dp", "tensor"), None), P())
    return jax.shard_map(shards, mesh=mesh, in_specs=in_specs, out_specs=out_specs, check_vma=False)
```

```python
import functools

import jax
import jax.numpy as jnp
from jax import lax
from jax.experimental import pallas as pl
from jax.experimental.pallas import tpu as pltpu
from jax.sharding import PartitionSpec as P

F32 = jnp.float32
BF16 = jnp.bfloat16
VMEM = pl.BlockSpec(memory_space=pltpu.VMEM)
MB = 1024 * 1024


def shape(dims, dtype):
    return jax.ShapeDtypeStruct(dims, dtype)


def split_high_low(value):
    high = value.astype(BF16)
    return high, (value - high.astype(F32)).astype(BF16)


def dot(a, b, ca=1, cb=0, precision=None):
    return lax.dot_general(
        a, b, (((ca,), (cb,)), ((), ())), preferred_element_type=F32, precision=precision
    )


def call(kernel, outs, *args, ins=None, out_specs=None, scratch=(), flops=0, moved=0, limit=16, **kw):
    many = isinstance(outs, tuple)
    return pl.pallas_call(
        kernel,
        out_shape=outs,
        in_specs=ins or [VMEM] * len(args),
        out_specs=out_specs or ((VMEM,) * len(outs) if many else VMEM),
        scratch_shapes=list(scratch),
        compiler_params=pltpu.CompilerParams(vmem_limit_bytes=limit * MB),
        cost_estimate=pl.CostEstimate(flops=flops, bytes_accessed=moved, transcendentals=0),
        **kw,
    )(*args)


def core_index():
    return lax.rem(lax.axis_index("dp"), 2)


def store_halves(value, mine_ref, other_ref):
    half = value.shape[1] // 2
    low = core_index() == 0
    left, right = value[:, :half], value[:, half:]
    mine_ref[...] = jnp.where(low, left, right)
    other_ref[...] = jnp.where(low, right, left)


def join_halves(mine, other):
    low = core_index() == 0
    return jnp.concatenate([jnp.where(low, mine, other), jnp.where(low, other, mine)], axis=1)


def token_kernel(cot_ref, warm_ref, out_ref):
    rank = warm_ref.shape[0]
    cot = cot_ref[...]
    warm_2 = jnp.concatenate(split_high_low(warm_ref[...]), axis=0)
    both = dot(cot, warm_2, 1, 1)
    both = jnp.concatenate(split_high_low(both[:, :rank] + both[:, rank:]), axis=1)
    for k in range(out_ref.shape[0]):
        out_ref[k] = both


def part_kernel(q_ref, attn_ref, e_ref, mine_ref, other_ref):
    rank = e_ref.shape[0]
    both = dot(q_ref[...], attn_ref[...], 0, 0)
    store_halves(both[:rank] + both[rank:] + e_ref[...], mine_ref, other_ref)


def spread_kernel(mine_ref, got_ref, out_ref):
    value = (mine_ref[...] + got_ref[...]).astype(BF16)
    for k in range(out_ref.shape[0]):
        out_ref[k] = value


def total_of(ref):
    value = ref[0].astype(F32)
    for k in range(1, ref.shape[0]):
        value = value + ref[k].astype(F32)
    return value


def mean_kernel(replicas, parts_ref, out_ref):
    out_ref[...] = total_of(parts_ref) * (1.0 / replicas)


def feature_kernel(mine_ref, other_ref, attn_ref, panel_ref, out_ref):
    rank = mine_ref.shape[0]
    panel = join_halves(mine_ref[...], other_ref[...])
    panel_ref[...] = panel
    panel_2 = jnp.concatenate(split_high_low(panel), axis=0)
    gram = dot(panel_2, panel_2, 1, 1)
    gram = gram[:rank, :rank] + gram[:rank, rank:] + gram[rank:, :rank] + gram[rank:, rank:]
    part = rank // 2
    gram = jnp.where(core_index() == 0, gram[:part], gram[part:])
    gram = jnp.concatenate(split_high_low(gram), axis=0)
    both = dot(attn_ref[...], panel_2, 1, 1)
    both = (both[:, :rank] + both[:, rank:]).astype(BF16)
    tok = both.shape[0] // out_ref.shape[0]
    for k in range(out_ref.shape[0]):
        out_ref[k, pl.ds(0, tok), pl.ds(0, rank)] = both[k * tok:(k + 1) * tok]
        out_ref[k, pl.ds(tok, rank - tok), pl.ds(0, rank)] = jnp.zeros((rank - tok, rank), BF16)
        out_ref[k, :, pl.ds(rank, rank)] = gram


def error_term_kernel(panel_ref, error_ref, out_ref):
    step = pl.program_id(0)
    rank, rows = panel_ref.shape[0], error_ref.shape[0]
    panel_2 = jnp.concatenate(split_high_low(panel_ref[...]), axis=0)
    for c in range(0, error_ref.shape[1], 1024):
        columns = pl.ds(c, 1024)
        both = dot(panel_2, error_ref[:, columns])
        both = both[:rank] + both[rank:]

        @pl.when(step == 0)
        def _():
            out_ref[:, columns] = both

        @pl.when(step > 0)
        def _():
            out_ref[:, columns] += both


def basis_term_kernel(parts_ref, cot_ref, error_term_ref, mine_ref, other_ref, gram_ref):
    tok, rank = cot_ref.shape[0], error_term_ref.shape[0]
    part = rank // 2
    value = total_of(parts_ref)
    gram_ref[...] = value[:part, rank:] + value[part:, rank:]
    token_2 = jnp.concatenate(split_high_low(value[:tok, :rank]), axis=1)
    both = dot(token_2, cot_ref[...], 0, 0)
    store_halves(both[:rank] + both[rank:] + error_term_ref[...], mine_ref, other_ref)


def pieces_kernel(mine_ref, got_ref, out_ref):
    for k in range(out_ref.shape[0]):
        columns = pl.ds(k * 128, 128)
        out_ref[k] = (mine_ref[:, columns] + got_ref[:, columns]).astype(BF16)


def sum_kernel(parts_ref, out_ref):
    piece = total_of(parts_ref).astype(BF16)
    for k in range(out_ref.shape[0]):
        out_ref[k] = piece


def inverse_kernel(mine_ref, other_ref, out_ref):
    rank = mine_ref.shape[1]
    low = core_index() == 0
    mine, other = mine_ref[...], other_ref[...]
    gram = jnp.concatenate([jnp.where(low, mine, other), jnp.where(low, other, mine)], axis=0)
    row_of = lax.broadcasted_iota(jnp.int32, (rank, rank), 0)
    column_of = lax.broadcasted_iota(jnp.int32, (rank, rank), 1)
    state = jnp.concatenate([gram, (row_of == column_of).astype(F32)], axis=1)
    rows = [state[8 * b:8 * b + 8] for b in range(rank // 8)]
    index = lax.broadcasted_iota(jnp.int32, (8, 2 * rank), 0)
    for k in range(rank):
        b, r = divmod(k, 8)
        pivot = rows[b][r:r + 1, k:k + 1]
        scale = lax.rsqrt(pivot)
        scale = scale * (1.5 - 0.5 * pivot * scale * scale)
        row = rows[b][r:r + 1] * scale
        for j in range(b, rank // 8):
            factor = rows[j][:, k:k + 1] * scale
            update = rows[j] - factor * row
            if j == b:
                rows[j] = jnp.where(index > r, update, jnp.where(index == r, row, rows[j]))
            else:
                rows[j] = update
    out_ref[...] = jnp.concatenate(rows, axis=0)[:, rank:]


def basis_kernel(replicas, parts_ref, inverse_ref, out_ref):
    value = total_of(parts_ref) * (1.0 / replicas)
    value = dot(inverse_ref[...], value, precision=lax.Precision.HIGHEST).astype(BF16)
    for k in range(out_ref.shape[0]):
        out_ref[k] = value


def ortho_kernel(panel_ref, inverse_ref, out_ref):
    value = dot(panel_ref[...], inverse_ref[...], 0, 1, lax.Precision.HIGHEST)
    out_ref[...] = jnp.concatenate(split_high_low(value), axis=1)


def columns_kernel(mine_ref, other_ref, twice_ref, basis_ref):
    rank = basis_ref.shape[0]
    low = core_index() == 0
    pieces = mine_ref.shape[0]
    for k in range(pieces):
        mine, other = mine_ref[k], other_ref[k]
        for place, value in ((k, jnp.where(low, mine, other)), (k + pieces, jnp.where(low, other, mine))):
            columns = pl.ds(place * 128, 128)
            twice_ref[pl.ds(0, rank), columns] = value
            twice_ref[pl.ds(rank, rank), columns] = value
            basis_ref[:, columns] = value.astype(F32)


def shards(attn, cot, weight, error, warm):
    dp = lax.axis_size("dp")
    group = lax.axis_size("tensor")
    zs = dp // 2
    rank = warm.shape[1]
    tokens, feats = attn.shape
    tok, width = cot.shape
    half = width // 2
    warm = warm.T
    pair = [(i, i ^ 1) for i in range(dp)]
    z_groups = [list(range(c, dp, 2)) for c in range(2)]
    barrier = lax.optimization_barrier

    def swap(value):
        return lax.ppermute(value, "dp", pair)

    def exchange(value, axis, groups=None):
        return lax.all_to_all(value, axis, 0, 0, tiled=True, axis_index_groups=groups)

    cot_all = lax.all_gather(cot, "tensor", axis=0, tiled=True)

    q = call(
        token_kernel, shape((group, tok, 2 * rank), BF16), cot, warm, flops=4 * tok * width * rank, moved=3 * MB
    )
    q = exchange(q, "tensor").reshape(tokens, 2 * rank)
    e = dot(jnp.concatenate(split_high_low(warm), axis=0), error, 1, 1)
    e = e[:rank] + e[rank:]
    q, e = barrier((q, e))
    half_panel = shape((rank, feats // 2), F32)
    mine, other = call(part_kernel, (half_panel, half_panel), q, attn, e, flops=2 * 128 * feats * tokens, moved=MB)
    spread = call(spread_kernel, shape((zs, rank, feats // 2), BF16), mine, swap(other), moved=MB // 2)
    parts = exchange(spread, "dp", z_groups)
    mine = call(functools.partial(mean_kernel, dp), half_panel, parts, moved=MB // 2)
    other = swap(mine)

    panel, packed = call(
        feature_kernel,
        (shape((rank, feats), F32), shape((group, rank, 2 * rank), BF16)),
        mine, other, attn, flops=4 * tokens * feats * rank, moved=2 * MB,
    )
    parts = exchange(packed, "tensor")
    rows = feats // 2
    error_term = call(
        error_term_kernel, shape((rank, width), F32), panel, error,
        grid=(feats // rows,),
        ins=[pl.BlockSpec((rank, rows), lambda i: (0, i)), pl.BlockSpec((rows, width), lambda i: (i, 0))],
        out_specs=pl.BlockSpec((rank, width), lambda i: (0, 0)),
        flops=4 * feats * width * rank, moved=6 * MB,
    )
    parts, error_term = barrier((parts, error_term))

    half_basis = shape((rank, half), F32)
    mine, other, gram = call(
        basis_term_kernel, (half_basis, half_basis, shape((rank // 2, rank), F32)), parts, cot, error_term, moved=4 * MB
    )
    packed = call(pieces_kernel, shape((group, rank, half // group), BF16), mine, swap(other), moved=2 * MB)
    parts = exchange(packed, "tensor")
    inverse = call(inverse_kernel, shape((rank, rank), F32), gram, swap(gram), flops=5 * 10**9, moved=MB // 16)
    ortho = call(ortho_kernel, shape((feats, 2 * rank), BF16), panel, inverse, flops=10**8, moved=MB // 4)
    parts, inverse, ortho = barrier((parts, inverse, ortho))
    spread = call(sum_kernel, shape((zs, rank, half // group), BF16), parts, moved=MB // 2)
    parts = exchange(spread, "dp", z_groups)
    grad_in = dot(cot_all, weight, 1, 1).astype(BF16)
    parts, grad_in = barrier((parts, grad_in))
    spread = call(
        functools.partial(basis_kernel, dp), shape((group, rank, half // group), BF16), parts, inverse, moved=MB // 2
    )
    mine = exchange(spread, "tensor")
    merged = (dot(attn, cot_all, 0, 0) + error.astype(F32)).astype(BF16)
    mine, merged = barrier((mine, merged))
    other = swap(mine)

    twice, new_basis = call(
        columns_kernel, (shape((2 * rank, width), BF16), shape((rank, width), F32)), mine, other, moved=3 * MB
    )
    new_error = (merged.astype(F32) - dot(ortho, twice)).astype(BF16)
    return grad_in, new_error, new_basis.T


def solution(mesh):
    in_specs = (
        P("dp", "tensor"),
        P(("dp", "tensor"), None),
        P("tensor", None),
        P(("dp", "tensor"), None),
        P(),
    )
    out_specs = (P("dp", "tensor"), P(("dp", "tensor"), None), P())
    return jax.shard_map(shards, mesh=mesh, in_specs=in_specs, out_specs=out_specs, check_vma=False)
```

```python
import functools

import jax
import jax.numpy as jnp
from jax import lax
from jax.experimental import pallas as pl
from jax.experimental.pallas import tpu as pltpu
from jax.sharding import PartitionSpec as P

F32 = jnp.float32
BF16 = jnp.bfloat16
VMEM = pl.BlockSpec(memory_space=pltpu.VMEM)
MB = 1024 * 1024


def shape(dims, dtype):
    return jax.ShapeDtypeStruct(dims, dtype)


def split_high_low(value):
    high = value.astype(BF16)
    return high, (value - high.astype(F32)).astype(BF16)


def dot(a, b, ca=1, cb=0, precision=None):
    return lax.dot_general(
        a, b, (((ca,), (cb,)), ((), ())), preferred_element_type=F32, precision=precision
    )


def call(kernel, outs, *args, ins=None, out_specs=None, scratch=(), flops=0, moved=0, limit=16, **kw):
    many = isinstance(outs, tuple)
    return pl.pallas_call(
        kernel,
        out_shape=outs,
        in_specs=ins or [VMEM] * len(args),
        out_specs=out_specs or ((VMEM,) * len(outs) if many else VMEM),
        scratch_shapes=list(scratch),
        compiler_params=pltpu.CompilerParams(vmem_limit_bytes=limit * MB),
        cost_estimate=pl.CostEstimate(flops=flops, bytes_accessed=moved, transcendentals=0),
        **kw,
    )(*args)


def core_index():
    return lax.rem(lax.axis_index("dp"), 2)


def store_halves(value, mine_ref, other_ref):
    half = value.shape[1] // 2
    low = core_index() == 0
    left, right = value[:, :half], value[:, half:]
    mine_ref[...] = jnp.where(low, left, right)
    other_ref[...] = jnp.where(low, right, left).astype(other_ref.dtype)


def join_halves(mine, other):
    low = core_index() == 0
    return jnp.concatenate([jnp.where(low, mine, other), jnp.where(low, other, mine)], axis=1)


def token_kernel(cot_hbm, warm_hbm, out_ref, cot_ref, warm_ref, sems):
    rank, width = warm_ref.shape
    chunk = width // 2
    copies = []
    for c in range(2):
        columns = pl.ds(c * chunk, chunk)
        copies.append([
            pltpu.make_async_copy(src.at[:, columns], dst.at[:, columns], sems.at[2 * c + k])
            for k, (src, dst) in enumerate(((warm_hbm, warm_ref), (cot_hbm, cot_ref)))
        ])
    for copy in copies[0] + copies[1]:
        copy.start()
    both = None
    for c in range(2):
        columns = pl.ds(c * chunk, chunk)
        for copy in copies[c]:
            copy.wait()
        warm_2 = jnp.concatenate(split_high_low(warm_ref[:, columns]), axis=0)
        term = dot(cot_ref[:, columns], warm_2, 1, 1)
        both = term if both is None else both + term
    both = jnp.concatenate(split_high_low(both[:, :rank] + both[:, rank:]), axis=1)
    for k in range(out_ref.shape[0]):
        out_ref[k] = both


def part_kernel(q_ref, attn_ref, e_ref, mine_ref, other_ref):
    rank = e_ref.shape[0]
    both = dot(q_ref[...], attn_ref[...], 0, 0)
    store_halves(both[:rank] + both[rank:] + e_ref[...], mine_ref, other_ref)


def spread_kernel(mine_ref, got_ref, out_ref):
    value = (mine_ref[...] + got_ref[...]).astype(BF16)
    for k in range(out_ref.shape[0]):
        out_ref[k] = value


def total_of(ref):
    value = ref[0].astype(F32)
    for k in range(1, ref.shape[0]):
        value = value + ref[k].astype(F32)
    return value


def mean_kernel(replicas, parts_ref, out_ref):
    out_ref[...] = total_of(parts_ref) * (1.0 / replicas)


def feature_kernel(mine_ref, other_ref, attn_ref, panel_ref, out_ref):
    rank = mine_ref.shape[0]
    panel = join_halves(mine_ref[...], other_ref[...])
    panel_ref[...] = panel
    panel_2 = jnp.concatenate(split_high_low(panel), axis=0)
    gram = dot(panel_2, panel_2, 1, 1)
    gram = gram[:rank, :rank] + gram[:rank, rank:] + gram[rank:, :rank] + gram[rank:, rank:]
    part = rank // 2
    gram = jnp.where(core_index() == 0, gram[:part], gram[part:])
    gram = jnp.concatenate(split_high_low(gram), axis=0)
    both = dot(attn_ref[...], panel_2, 1, 1)
    both = (both[:, :rank] + both[:, rank:]).astype(BF16)
    tok = both.shape[0] // out_ref.shape[0]
    for k in range(out_ref.shape[0]):
        out_ref[k, pl.ds(0, tok), pl.ds(0, rank)] = both[k * tok:(k + 1) * tok]
        out_ref[k, pl.ds(tok, rank - tok), pl.ds(0, rank)] = jnp.zeros((rank - tok, rank), BF16)
        out_ref[k, :, pl.ds(rank, rank)] = gram


def error_term_kernel(panel_ref, error_ref, out_ref):
    step = pl.program_id(0)
    rank, rows = panel_ref.shape[0], error_ref.shape[0]
    panel_2 = jnp.concatenate(split_high_low(panel_ref[...]), axis=0)
    for c in range(0, error_ref.shape[1], 1024):
        columns = pl.ds(c, 1024)
        both = dot(panel_2, error_ref[:, columns])
        both = both[:rank] + both[rank:]

        @pl.when(step == 0)
        def _():
            out_ref[:, columns] = both

        @pl.when(step > 0)
        def _():
            out_ref[:, columns] += both


def basis_term_kernel(parts_ref, cot_ref, error_term_ref, mine_ref, other_ref, gram_ref):
    tok, rank = cot_ref.shape[0], error_term_ref.shape[0]
    part = rank // 2
    value = total_of(parts_ref)
    gram_ref[...] = value[:part, rank:] + value[part:, rank:]
    token_2 = jnp.concatenate(split_high_low(value[:tok, :rank]), axis=1)
    both = dot(token_2, cot_ref[...], 0, 0)
    store_halves(both[:rank] + both[rank:] + error_term_ref[...], mine_ref, other_ref)


def pieces_kernel(mine_ref, got_ref, out_ref):
    for k in range(out_ref.shape[0]):
        columns = pl.ds(k * 128, 128)
        out_ref[k] = (mine_ref[:, columns] + got_ref[:, columns].astype(F32)).astype(BF16)


def sum_kernel(parts_ref, out_ref):
    piece = total_of(parts_ref).astype(BF16)
    for k in range(out_ref.shape[0]):
        out_ref[k] = piece


def inverse_kernel(mine_ref, other_ref, out_ref):
    rank = mine_ref.shape[1]
    low = core_index() == 0
    mine, other = mine_ref[...], other_ref[...]
    gram = jnp.concatenate([jnp.where(low, mine, other), jnp.where(low, other, mine)], axis=0)
    row_of = lax.broadcasted_iota(jnp.int32, (rank, rank), 0)
    column_of = lax.broadcasted_iota(jnp.int32, (rank, rank), 1)
    state = jnp.concatenate([gram, (row_of == column_of).astype(F32)], axis=1)
    rows = [state[8 * b:8 * b + 8] for b in range(rank // 8)]
    index = lax.broadcasted_iota(jnp.int32, (8, 2 * rank), 0)
    for k in range(rank):
        b, r = divmod(k, 8)
        pivot = rows[b][r:r + 1, k:k + 1]
        scale = lax.rsqrt(pivot)
        scale = scale * (1.5 - 0.5 * pivot * scale * scale)
        row = rows[b][r:r + 1] * scale
        for j in range(b, rank // 8):
            factor = rows[j][:, k:k + 1] * scale
            update = rows[j] - factor * row
            if j == b:
                rows[j] = jnp.where(index > r, update, jnp.where(index == r, row, rows[j]))
            else:
                rows[j] = update
    out_ref[...] = jnp.concatenate(rows, axis=0)[:, rank:]


def basis_kernel(replicas, parts_ref, inverse_ref, out_ref):
    value = total_of(parts_ref) * (1.0 / replicas)
    value = dot(inverse_ref[...], value, precision=lax.Precision.HIGHEST).astype(BF16)
    for k in range(out_ref.shape[0]):
        out_ref[k] = value


def ortho_kernel(panel_ref, inverse_ref, out_ref):
    out_ref[...] = dot(panel_ref[...], inverse_ref[...], 0, 1, lax.Precision.HIGHEST).astype(BF16)


def final_kernel(mine_ref, other_ref, ortho_ref, merged_ref, error_ref, basis_ref, basis):
    @pl.when(pl.program_id(0) == 0)
    def _():
        low = core_index() == 0
        pieces = mine_ref.shape[0]
        for k in range(pieces):
            mine, other = mine_ref[k], other_ref[k]
            for place, value in ((k, jnp.where(low, mine, other)), (k + pieces, jnp.where(low, other, mine))):
                columns = pl.ds(place * 128, 128)
                basis[:, columns] = value
                basis_ref[:, columns] = value.astype(F32)

    for c in range(0, error_ref.shape[1], 1024):
        columns = pl.ds(c, 1024)
        approx = dot(ortho_ref[...], basis[:, columns])
        error_ref[:, columns] = (merged_ref[:, columns].astype(F32) - approx).astype(BF16)


def shards(attn, cot, weight, error, warm):
    dp = lax.axis_size("dp")
    group = lax.axis_size("tensor")
    zs = dp // 2
    rank = warm.shape[1]
    tokens, feats = attn.shape
    tok, width = cot.shape
    half = width // 2
    warm = warm.T
    pair = [(i, i ^ 1) for i in range(dp)]
    z_groups = [list(range(0, dp, 2)), list(range(dp - 1, 0, -2))]
    barrier = lax.optimization_barrier

    def swap(value):
        return lax.ppermute(value, "dp", pair)

    def exchange(value, axis, groups=None):
        return lax.all_to_all(value, axis, 0, 0, tiled=True, axis_index_groups=groups)

    cot_all = lax.all_gather(cot, "tensor", axis=0, tiled=True)

    anywhere = pl.BlockSpec(memory_space=pl.ANY)
    q = call(
        token_kernel, shape((group, tok, 2 * rank), BF16), cot, warm,
        ins=[anywhere, anywhere],
        scratch=[pltpu.VMEM((tok, width), BF16), pltpu.VMEM((rank, width), F32), pltpu.SemaphoreType.DMA((4,))],
        flops=4 * tok * width * rank, moved=3 * MB, limit=60,
    )
    q = exchange(q, "tensor").reshape(tokens, 2 * rank)
    e = dot(jnp.concatenate(split_high_low(warm), axis=0), error, 1, 1)
    e = e[:rank] + e[rank:]
    q, e = barrier((q, e))
    half_panel = shape((rank, feats // 2), F32)
    mine, other = call(part_kernel, (half_panel, half_panel), q, attn, e, flops=2 * 128 * feats * tokens, moved=MB)
    spread = call(spread_kernel, shape((zs, rank, feats // 2), BF16), mine, swap(other), moved=MB // 2)
    parts = exchange(spread, "dp", z_groups)
    mine = call(functools.partial(mean_kernel, dp), half_panel, parts, moved=MB // 2)
    other = swap(mine)

    panel, packed = call(
        feature_kernel,
        (shape((rank, feats), F32), shape((group, rank, 2 * rank), BF16)),
        mine, other, attn, flops=4 * tokens * feats * rank, moved=2 * MB,
    )
    parts = exchange(packed, "tensor")
    rows = feats // 2
    error_term = call(
        error_term_kernel, shape((rank, width), F32), panel, error,
        grid=(feats // rows,),
        ins=[pl.BlockSpec((rank, rows), lambda i: (0, i)), pl.BlockSpec((rows, width), lambda i: (i, 0))],
        out_specs=pl.BlockSpec((rank, width), lambda i: (0, 0)),
        flops=4 * feats * width * rank, moved=6 * MB,
    )
    parts, error_term = barrier((parts, error_term))

    half_basis = shape((rank, half), F32)
    mine, other, gram = call(
        basis_term_kernel, (half_basis, shape((rank, half), BF16), shape((rank // 2, rank), F32)), parts, cot, error_term, moved=4 * MB
    )
    packed = call(pieces_kernel, shape((group, rank, half // group), BF16), mine, swap(other), moved=2 * MB)
    parts = exchange(packed, "tensor")
    inverse = call(inverse_kernel, shape((rank, rank), F32), gram, swap(gram), flops=5 * 10**9, moved=MB // 16)
    ortho = call(ortho_kernel, shape((feats, rank), BF16), panel, inverse, flops=10**8, moved=MB // 4)
    parts, inverse, ortho = barrier((parts, inverse, ortho))
    spread = call(sum_kernel, shape((zs, rank, half // group), BF16), parts, moved=MB // 2)
    parts = exchange(spread, "dp", z_groups)
    grad_in = dot(cot_all, weight, 1, 1).astype(BF16)
    parts, grad_in = barrier((parts, grad_in))
    spread = call(
        functools.partial(basis_kernel, dp), shape((group, rank, half // group), BF16), parts, inverse, moved=MB // 2
    )
    mine = exchange(spread, "tensor")
    merged = (dot(attn, cot_all, 0, 0) + error.astype(F32)).astype(BF16)
    mine, merged = barrier((mine, merged))
    other = swap(mine)
    rows = feats // 2
    new_error, new_basis = call(
        final_kernel,
        (shape((feats, width), BF16), shape((rank, width), F32)),
        mine, other, ortho, merged,
        grid=(feats // rows,),
        ins=[pl.BlockSpec(mine.shape, lambda i: (0, 0, 0))] * 2
        + [pl.BlockSpec((rows, rank), lambda i: (i, 0)), pl.BlockSpec((rows, width), lambda i: (i, 0))],
        out_specs=(pl.BlockSpec((rows, width), lambda i: (i, 0)), pl.BlockSpec((rank, width), lambda i: (0, 0))),
        scratch=[pltpu.VMEM((rank, width), BF16)],
        flops=2 * feats * width * rank, moved=10 * MB, limit=60,
    )
    return grad_in, new_error, new_basis.T


def solution(mesh):
    in_specs = (
        P("dp", "tensor"),
        P(("dp", "tensor"), None),
        P("tensor", None),
        P(("dp", "tensor"), None),
        P(),
    )
    out_specs = (P("dp", "tensor"), P(("dp", "tensor"), None), P())
    return jax.shard_map(shards, mesh=mesh, in_specs=in_specs, out_specs=out_specs, check_vma=False)
```

```python
import functools

import jax
import jax.numpy as jnp
from jax import lax
from jax.experimental import pallas as pl
from jax.experimental.pallas import tpu as pltpu
from jax.sharding import PartitionSpec as P

F32 = jnp.float32
BF16 = jnp.bfloat16
VMEM = pl.BlockSpec(memory_space=pltpu.VMEM)
MB = 1024 * 1024


def shape(dims, dtype):
    return jax.ShapeDtypeStruct(dims, dtype)


def split_high_low(value):
    high = value.astype(BF16)
    return high, (value - high.astype(F32)).astype(BF16)


def dot(a, b, ca=1, cb=0, precision=None):
    return lax.dot_general(
        a, b, (((ca,), (cb,)), ((), ())), preferred_element_type=F32, precision=precision
    )


def call(kernel, outs, *args, ins=None, out_specs=None, scratch=(), flops=0, moved=0, limit=16, **kw):
    many = isinstance(outs, tuple)
    return pl.pallas_call(
        kernel,
        out_shape=outs,
        in_specs=ins or [VMEM] * len(args),
        out_specs=out_specs or ((VMEM,) * len(outs) if many else VMEM),
        scratch_shapes=list(scratch),
        compiler_params=pltpu.CompilerParams(vmem_limit_bytes=limit * MB),
        cost_estimate=pl.CostEstimate(flops=flops, bytes_accessed=moved, transcendentals=0),
        **kw,
    )(*args)


def core_index():
    return lax.rem(lax.axis_index("dp"), 2)


def store_halves(value, mine_ref, other_ref):
    half = value.shape[1] // 2
    low = core_index() == 0
    left, right = value[:, :half], value[:, half:]
    mine_ref[...] = jnp.where(low, left, right)
    other_ref[...] = jnp.where(low, right, left).astype(other_ref.dtype)


def join_halves(mine, other):
    low = core_index() == 0
    return jnp.concatenate([jnp.where(low, mine, other), jnp.where(low, other, mine)], axis=1)


def token_kernel(cot_hbm, warm_hbm, out_ref, cot_ref, warm_ref, sems):
    rank, width = warm_ref.shape
    chunk = width // 2
    copies = []
    for c in range(2):
        columns = pl.ds(c * chunk, chunk)
        copies.append([
            pltpu.make_async_copy(src.at[:, columns], dst.at[:, columns], sems.at[2 * c + k])
            for k, (src, dst) in enumerate(((warm_hbm, warm_ref), (cot_hbm, cot_ref)))
        ])
    for copy in copies[0] + copies[1]:
        copy.start()
    both = None
    for c in range(2):
        columns = pl.ds(c * chunk, chunk)
        for copy in copies[c]:
            copy.wait()
        warm_2 = jnp.concatenate(split_high_low(warm_ref[:, columns]), axis=0)
        term = dot(cot_ref[:, columns], warm_2, 1, 1)
        both = term if both is None else both + term
    both = jnp.concatenate(split_high_low(both[:, :rank] + both[:, rank:]), axis=1)
    for k in range(out_ref.shape[0]):
        out_ref[k] = both


def part_kernel(q_ref, attn_ref, e_ref, mine_ref, other_ref):
    rank = e_ref.shape[0]
    both = dot(q_ref[...], attn_ref[...], 0, 0)
    store_halves(both[:rank] + both[rank:] + e_ref[...], mine_ref, other_ref)


def spread_kernel(mine_ref, got_ref, out_ref):
    value = (mine_ref[...] + got_ref[...]).astype(BF16)
    for k in range(out_ref.shape[0]):
        out_ref[k] = value


def total_of(ref):
    value = ref[0].astype(F32)
    for k in range(1, ref.shape[0]):
        value = value + ref[k].astype(F32)
    return value


def mean_kernel(replicas, parts_ref, out_ref):
    out_ref[...] = total_of(parts_ref) * (1.0 / replicas)


def feature_kernel(mine_ref, other_ref, attn_ref, panel_ref, out_ref):
    rank = mine_ref.shape[0]
    panel = join_halves(mine_ref[...], other_ref[...])
    panel_ref[...] = panel
    panel_2 = jnp.concatenate(split_high_low(panel), axis=0)
    gram = dot(panel_2, panel_2, 1, 1)
    gram = gram[:rank, :rank] + gram[:rank, rank:] + gram[rank:, :rank] + gram[rank:, rank:]
    part = rank // 2
    gram = jnp.where(core_index() == 0, gram[:part], gram[part:])
    gram = jnp.concatenate(split_high_low(gram), axis=0)
    both = dot(attn_ref[...], panel_2, 1, 1)
    both = (both[:, :rank] + both[:, rank:]).astype(BF16)
    tok = both.shape[0] // out_ref.shape[0]
    for k in range(out_ref.shape[0]):
        out_ref[k, pl.ds(0, tok), pl.ds(0, rank)] = both[k * tok:(k + 1) * tok]
        out_ref[k, pl.ds(tok, rank - tok), pl.ds(0, rank)] = jnp.zeros((rank - tok, rank), BF16)
        out_ref[k, :, pl.ds(rank, rank)] = gram


def error_term_kernel(panel_ref, error_ref, out_ref):
    step = pl.program_id(0)
    rank, rows = panel_ref.shape[0], error_ref.shape[0]
    panel_2 = jnp.concatenate(split_high_low(panel_ref[...]), axis=0)
    for c in range(0, error_ref.shape[1], 1024):
        columns = pl.ds(c, 1024)
        both = dot(panel_2, error_ref[:, columns])
        both = both[:rank] + both[rank:]

        @pl.when(step == 0)
        def _():
            out_ref[:, columns] = both

        @pl.when(step > 0)
        def _():
            out_ref[:, columns] += both


def basis_term_kernel(parts_ref, cot_ref, error_term_ref, mine_ref, other_ref, gram_ref):
    tok, rank = cot_ref.shape[0], error_term_ref.shape[0]
    part = rank // 2
    value = total_of(parts_ref)
    gram_ref[...] = value[:part, rank:] + value[part:, rank:]
    token_2 = jnp.concatenate(split_high_low(value[:tok, :rank]), axis=1)
    both = dot(token_2, cot_ref[...], 0, 0)
    store_halves(both[:rank] + both[rank:] + error_term_ref[...], mine_ref, other_ref)


def pieces_kernel(mine_ref, got_ref, out_ref):
    for k in range(out_ref.shape[0]):
        columns = pl.ds(k * 128, 128)
        out_ref[k] = (mine_ref[:, columns] + got_ref[:, columns].astype(F32)).astype(BF16)


def sum_kernel(parts_ref, out_ref):
    piece = total_of(parts_ref).astype(BF16)
    for k in range(out_ref.shape[0]):
        out_ref[k] = piece


def inverse_kernel(mine_ref, other_ref, out_ref):
    rank = mine_ref.shape[1]
    low = core_index() == 0
    mine, other = mine_ref[...], other_ref[...]
    gram = jnp.concatenate([jnp.where(low, mine, other), jnp.where(low, other, mine)], axis=0)
    row_of = lax.broadcasted_iota(jnp.int32, (rank, rank), 0)
    column_of = lax.broadcasted_iota(jnp.int32, (rank, rank), 1)
    state = jnp.concatenate([gram, (row_of == column_of).astype(F32)], axis=1)
    rows = [state[8 * b:8 * b + 8] for b in range(rank // 8)]
    index = lax.broadcasted_iota(jnp.int32, (8, 2 * rank), 0)
    for k in range(rank):
        b, r = divmod(k, 8)
        pivot = rows[b][r:r + 1, k:k + 1]
        scale = lax.rsqrt(pivot)
        scale = scale * (1.5 - 0.5 * pivot * scale * scale)
        row = rows[b][r:r + 1] * scale
        for j in range(b, rank // 8):
            factor = rows[j][:, k:k + 1] * scale
            update = rows[j] - factor * row
            if j == b:
                rows[j] = jnp.where(index > r, update, jnp.where(index == r, row, rows[j]))
            else:
                rows[j] = update
    out_ref[...] = jnp.concatenate(rows, axis=0)[:, rank:]


def basis_kernel(replicas, parts_ref, inverse_ref, out_ref):
    value = total_of(parts_ref) * (1.0 / replicas)
    value = dot(inverse_ref[...], value, precision=lax.Precision.HIGHEST).astype(BF16)
    for k in range(out_ref.shape[0]):
        out_ref[k] = value


def ortho_kernel(panel_ref, inverse_ref, out_ref):
    out_ref[...] = dot(panel_ref[...], inverse_ref[...], 0, 1, lax.Precision.HIGHEST).astype(BF16)


def final_kernel(mine_ref, other_ref, ortho_ref, merged_ref, error_ref, basis_ref, basis):
    @pl.when(pl.program_id(0) == 0)
    def _():
        low = core_index() == 0
        pieces = mine_ref.shape[0]
        for k in range(pieces):
            mine, other = mine_ref[k], other_ref[k]
            for place, value in ((k, jnp.where(low, mine, other)), (k + pieces, jnp.where(low, other, mine))):
                columns = pl.ds(place * 128, 128)
                basis[:, columns] = value
                basis_ref[:, columns] = value.astype(F32)

    for c in range(0, error_ref.shape[1], 1024):
        columns = pl.ds(c, 1024)
        approx = dot(ortho_ref[...], basis[:, columns])
        error_ref[:, columns] = (merged_ref[:, columns].astype(F32) - approx).astype(BF16)


def shards(attn, cot, weight, error, warm):
    dp = lax.axis_size("dp")
    group = lax.axis_size("tensor")
    zs = dp // 2
    rank = warm.shape[1]
    tokens, feats = attn.shape
    tok, width = cot.shape
    half = width // 2
    warm = warm.T
    pair = [(i, i ^ 1) for i in range(dp)]
    z_up = [list(range(c, dp, 2)) for c in range(2)]
    z_down = [planes[::-1] for planes in z_up]
    barrier = lax.optimization_barrier

    def swap(value):
        return lax.ppermute(value, "dp", pair)

    def exchange(value, axis, groups=None):
        return lax.all_to_all(value, axis, 0, 0, tiled=True, axis_index_groups=groups)

    cot_all = lax.all_gather(cot, "tensor", axis=0, tiled=True)

    anywhere = pl.BlockSpec(memory_space=pl.ANY)
    q = call(
        token_kernel, shape((group, tok, 2 * rank), BF16), cot, warm,
        ins=[anywhere, anywhere],
        scratch=[pltpu.VMEM((tok, width), BF16), pltpu.VMEM((rank, width), F32), pltpu.SemaphoreType.DMA((4,))],
        flops=4 * tok * width * rank, moved=3 * MB, limit=60,
    )
    q = exchange(q, "tensor").reshape(tokens, 2 * rank)
    e = dot(jnp.concatenate(split_high_low(warm), axis=0), error, 1, 1)
    e = e[:rank] + e[rank:]
    q, e = barrier((q, e))
    half_panel = shape((rank, feats // 2), F32)
    mine, other = call(part_kernel, (half_panel, half_panel), q, attn, e, flops=2 * 128 * feats * tokens, moved=MB)
    spread = call(spread_kernel, shape((zs, rank, feats // 2), BF16), mine, swap(other), moved=MB // 2)
    parts = exchange(spread, "dp", z_down)
    mine = call(functools.partial(mean_kernel, dp), half_panel, parts, moved=MB // 2)
    other = swap(mine)

    panel, packed = call(
        feature_kernel,
        (shape((rank, feats), F32), shape((group, rank, 2 * rank), BF16)),
        mine, other, attn, flops=4 * tokens * feats * rank, moved=2 * MB,
    )
    parts = exchange(packed, "tensor")
    rows = feats // 2
    error_term = call(
        error_term_kernel, shape((rank, width), F32), panel, error,
        grid=(feats // rows,),
        ins=[pl.BlockSpec((rank, rows), lambda i: (0, i)), pl.BlockSpec((rows, width), lambda i: (i, 0))],
        out_specs=pl.BlockSpec((rank, width), lambda i: (0, 0)),
        flops=4 * feats * width * rank, moved=6 * MB,
    )
    parts, error_term = barrier((parts, error_term))

    half_basis = shape((rank, half), F32)
    mine, other, gram = call(
        basis_term_kernel, (half_basis, shape((rank, half), BF16), shape((rank // 2, rank), F32)), parts, cot, error_term, moved=4 * MB
    )
    packed = call(pieces_kernel, shape((group, rank, half // group), BF16), mine, swap(other), moved=2 * MB)
    parts = exchange(packed, "tensor")
    inverse = call(inverse_kernel, shape((rank, rank), F32), gram, swap(gram), flops=5 * 10**9, moved=MB // 16)
    ortho = call(ortho_kernel, shape((feats, rank), BF16), panel, inverse, flops=10**8, moved=MB // 4)
    parts, inverse, ortho = barrier((parts, inverse, ortho))
    spread = call(sum_kernel, shape((zs, rank, half // group), BF16), parts, moved=MB // 2)
    parts = exchange(spread, "dp", z_up)
    grad_in = dot(cot_all, weight, 1, 1).astype(BF16)
    parts, grad_in = barrier((parts, grad_in))
    spread = call(
        functools.partial(basis_kernel, dp), shape((group, rank, half // group), BF16), parts, inverse, moved=MB // 2
    )
    mine = exchange(spread, "tensor")
    merged = (dot(attn, cot_all, 0, 0) + error.astype(F32)).astype(BF16)
    mine, merged = barrier((mine, merged))
    other = swap(mine)
    rows = feats // 2
    new_error, new_basis = call(
        final_kernel,
        (shape((feats, width), BF16), shape((rank, width), F32)),
        mine, other, ortho, merged,
        grid=(feats // rows,),
        ins=[pl.BlockSpec(mine.shape, lambda i: (0, 0, 0))] * 2
        + [pl.BlockSpec((rows, rank), lambda i: (i, 0)), pl.BlockSpec((rows, width), lambda i: (i, 0))],
        out_specs=(pl.BlockSpec((rows, width), lambda i: (i, 0)), pl.BlockSpec((rank, width), lambda i: (0, 0))),
        scratch=[pltpu.VMEM((rank, width), BF16)],
        flops=2 * feats * width * rank, moved=10 * MB, limit=60,
    )
    return grad_in, new_error, new_basis.T


def solution(mesh):
    in_specs = (
        P("dp", "tensor"),
        P(("dp", "tensor"), None),
        P("tensor", None),
        P(("dp", "tensor"), None),
        P(),
    )
    out_specs = (P("dp", "tensor"), P(("dp", "tensor"), None), P())
    return jax.shard_map(shards, mesh=mesh, in_specs=in_specs, out_specs=out_specs, check_vma=False)
```

```python
import functools

import jax
import jax.numpy as jnp
from jax import lax
from jax.experimental import pallas as pl
from jax.experimental.pallas import tpu as pltpu
from jax.sharding import PartitionSpec as P

F32 = jnp.float32
BF16 = jnp.bfloat16
VMEM = pl.BlockSpec(memory_space=pltpu.VMEM)
MB = 1024 * 1024


def shape(dims, dtype):
    return jax.ShapeDtypeStruct(dims, dtype)


def split_high_low(value):
    high = value.astype(BF16)
    return high, (value - high.astype(F32)).astype(BF16)


def dot(a, b, ca=1, cb=0, precision=None):
    return lax.dot_general(
        a, b, (((ca,), (cb,)), ((), ())), preferred_element_type=F32, precision=precision
    )


def call(kernel, outs, *args, ins=None, out_specs=None, scratch=(), flops=0, moved=0, limit=16, **kw):
    many = isinstance(outs, tuple)
    return pl.pallas_call(
        kernel,
        out_shape=outs,
        in_specs=ins or [VMEM] * len(args),
        out_specs=out_specs or ((VMEM,) * len(outs) if many else VMEM),
        scratch_shapes=list(scratch),
        compiler_params=pltpu.CompilerParams(vmem_limit_bytes=limit * MB),
        cost_estimate=pl.CostEstimate(flops=flops, bytes_accessed=moved, transcendentals=0),
        **kw,
    )(*args)


def core_index():
    return lax.rem(lax.axis_index("dp"), 2)


def store_halves(value, mine_ref, other_ref):
    half = value.shape[1] // 2
    low = core_index() == 0
    left, right = value[:, :half], value[:, half:]
    mine_ref[...] = jnp.where(low, left, right)
    other_ref[...] = jnp.where(low, right, left).astype(other_ref.dtype)


def join_halves(mine, other):
    low = core_index() == 0
    return jnp.concatenate([jnp.where(low, mine, other), jnp.where(low, other, mine)], axis=1)


def token_kernel(cot_hbm, warm_hbm, out_ref, cot_ref, warm_ref, sems):
    rank, width = warm_ref.shape
    chunk = width // 2
    copies = []
    for c in range(2):
        columns = pl.ds(c * chunk, chunk)
        copies.append([
            pltpu.make_async_copy(src.at[:, columns], dst.at[:, columns], sems.at[2 * c + k])
            for k, (src, dst) in enumerate(((warm_hbm, warm_ref), (cot_hbm, cot_ref)))
        ])
    for copy in copies[0] + copies[1]:
        copy.start()
    both = None
    for c in range(2):
        columns = pl.ds(c * chunk, chunk)
        for copy in copies[c]:
            copy.wait()
        warm_2 = jnp.concatenate(split_high_low(warm_ref[:, columns]), axis=0)
        term = dot(cot_ref[:, columns], warm_2, 1, 1)
        both = term if both is None else both + term
    both = jnp.concatenate(split_high_low(both[:, :rank] + both[:, rank:]), axis=1)
    for k in range(out_ref.shape[0]):
        out_ref[k] = both


def part_kernel(q_ref, attn_ref, e_ref, mine_ref, other_ref):
    rank = e_ref.shape[0]
    both = dot(q_ref[...], attn_ref[...], 0, 0)
    store_halves(both[:rank] + both[rank:] + e_ref[...], mine_ref, other_ref)


def spread_kernel(mine_ref, got_ref, out_ref):
    value = (mine_ref[...] + got_ref[...]).astype(BF16)
    for k in range(out_ref.shape[0]):
        out_ref[k] = value


def total_of(ref):
    value = ref[0].astype(F32)
    for k in range(1, ref.shape[0]):
        value = value + ref[k].astype(F32)
    return value


def mean_kernel(replicas, parts_ref, out_ref):
    out_ref[...] = total_of(parts_ref) * (1.0 / replicas)


def feature_kernel(mine_ref, other_ref, attn_ref, panel_ref, out_ref):
    rank = mine_ref.shape[0]
    panel = join_halves(mine_ref[...], other_ref[...])
    panel_ref[...] = panel
    panel_2 = jnp.concatenate(split_high_low(panel), axis=0)
    gram = dot(panel_2, panel_2, 1, 1)
    gram = gram[:rank, :rank] + gram[:rank, rank:] + gram[rank:, :rank] + gram[rank:, rank:]
    part = rank // 2
    gram = jnp.where(core_index() == 0, gram[:part], gram[part:])
    gram = jnp.concatenate(split_high_low(gram), axis=0)
    both = dot(attn_ref[...], panel_2, 1, 1)
    both = (both[:, :rank] + both[:, rank:]).astype(BF16)
    tok = both.shape[0] // out_ref.shape[0]
    for k in range(out_ref.shape[0]):
        out_ref[k, pl.ds(0, tok), pl.ds(0, rank)] = both[k * tok:(k + 1) * tok]
        out_ref[k, pl.ds(tok, rank - tok), pl.ds(0, rank)] = jnp.zeros((rank - tok, rank), BF16)
        out_ref[k, :, pl.ds(rank, rank)] = gram


def error_term_kernel(panel_ref, error_ref, out_ref):
    step = pl.program_id(0)
    rank, rows = panel_ref.shape[0], error_ref.shape[0]
    panel_2 = jnp.concatenate(split_high_low(panel_ref[...]), axis=0)
    for c in range(0, error_ref.shape[1], 1024):
        columns = pl.ds(c, 1024)
        both = dot(panel_2, error_ref[:, columns])
        both = both[:rank] + both[rank:]

        @pl.when(step == 0)
        def _():
            out_ref[:, columns] = both

        @pl.when(step > 0)
        def _():
            out_ref[:, columns] += both


def basis_term_kernel(parts_ref, cot_ref, error_term_ref, mine_ref, other_ref, gram_ref):
    tok, rank = cot_ref.shape[0], error_term_ref.shape[0]
    part = rank // 2
    value = total_of(parts_ref)
    gram_ref[...] = value[:part, rank:] + value[part:, rank:]
    token_2 = jnp.concatenate(split_high_low(value[:tok, :rank]), axis=1)
    both = dot(token_2, cot_ref[...], 0, 0)
    store_halves(both[:rank] + both[rank:] + error_term_ref[...], mine_ref, other_ref)


def pieces_kernel(mine_ref, got_ref, out_ref):
    for k in range(out_ref.shape[0]):
        columns = pl.ds(k * 128, 128)
        out_ref[k] = (mine_ref[:, columns] + got_ref[:, columns].astype(F32)).astype(BF16)


def sum_kernel(parts_ref, out_ref):
    piece = total_of(parts_ref).astype(BF16)
    for k in range(out_ref.shape[0]):
        out_ref[k] = piece


def inverse_kernel(mine_ref, other_ref, out_ref):
    rank = mine_ref.shape[1]
    low = core_index() == 0
    mine, other = mine_ref[...], other_ref[...]
    gram = jnp.concatenate([jnp.where(low, mine, other), jnp.where(low, other, mine)], axis=0)
    row_of = lax.broadcasted_iota(jnp.int32, (rank, rank), 0)
    column_of = lax.broadcasted_iota(jnp.int32, (rank, rank), 1)
    state = jnp.concatenate([gram, (row_of == column_of).astype(F32)], axis=1)
    rows = [state[8 * b:8 * b + 8] for b in range(rank // 8)]
    index = lax.broadcasted_iota(jnp.int32, (8, 2 * rank), 0)
    for k in range(rank):
        b, r = divmod(k, 8)
        pivot = rows[b][r:r + 1, k:k + 1]
        scale = lax.rsqrt(pivot)
        scale = scale * (1.5 - 0.5 * pivot * scale * scale)
        row = rows[b][r:r + 1] * scale
        for j in range(b, rank // 8):
            factor = rows[j][:, k:k + 1] * scale
            update = rows[j] - factor * row
            if j == b:
                rows[j] = jnp.where(index > r, update, jnp.where(index == r, row, rows[j]))
            else:
                rows[j] = update
    out_ref[...] = jnp.concatenate(rows, axis=0)[:, rank:]


def basis_kernel(replicas, parts_ref, inverse_ref, out_ref):
    value = total_of(parts_ref) * (1.0 / replicas)
    value = dot(inverse_ref[...], value, precision=lax.Precision.HIGHEST).astype(BF16)
    for k in range(out_ref.shape[0]):
        out_ref[k] = value


def ortho_kernel(panel_ref, inverse_ref, out_ref):
    out_ref[...] = dot(panel_ref[...], inverse_ref[...], 0, 1, lax.Precision.HIGHEST).astype(BF16)


def final_kernel(mine_hbm, other_hbm, ortho_ref, merged_ref, error_ref, basis_ref, basis, mine_ref, other_ref, sems):
    @pl.when(pl.program_id(0) == 0)
    def _():
        copies = [
            pltpu.make_async_copy(src, dst, sems.at[k])
            for k, (src, dst) in enumerate(((mine_hbm, mine_ref), (other_hbm, other_ref)))
        ]
        for copy in copies:
            copy.start()
        for copy in copies:
            copy.wait()
        low = core_index() == 0
        pieces = mine_ref.shape[0]
        for k in range(pieces):
            mine, other = mine_ref[k], other_ref[k]
            for place, value in ((k, jnp.where(low, mine, other)), (k + pieces, jnp.where(low, other, mine))):
                columns = pl.ds(place * 128, 128)
                basis[:, columns] = value
                basis_ref[:, columns] = value.astype(F32)

    for c in range(0, error_ref.shape[1], 1024):
        columns = pl.ds(c, 1024)
        approx = dot(ortho_ref[...], basis[:, columns])
        error_ref[:, columns] = (merged_ref[:, columns].astype(F32) - approx).astype(BF16)


def shards(attn, cot, weight, error, warm):
    dp = lax.axis_size("dp")
    group = lax.axis_size("tensor")
    zs = dp // 2
    rank = warm.shape[1]
    tokens, feats = attn.shape
    tok, width = cot.shape
    half = width // 2
    warm = warm.T
    pair = [(i, i ^ 1) for i in range(dp)]
    z_up = [list(range(c, dp, 2)) for c in range(2)]
    z_down = [planes[::-1] for planes in z_up]
    barrier = lax.optimization_barrier

    def swap(value):
        return lax.ppermute(value, "dp", pair)

    def exchange(value, axis, groups=None):
        return lax.all_to_all(value, axis, 0, 0, tiled=True, axis_index_groups=groups)

    cot_all = lax.all_gather(cot, "tensor", axis=0, tiled=True)

    anywhere = pl.BlockSpec(memory_space=pl.ANY)
    q = call(
        token_kernel, shape((group, tok, 2 * rank), BF16), cot, warm,
        ins=[anywhere, anywhere],
        scratch=[pltpu.VMEM((tok, width), BF16), pltpu.VMEM((rank, width), F32), pltpu.SemaphoreType.DMA((4,))],
        flops=4 * tok * width * rank, moved=3 * MB, limit=60,
    )
    q = exchange(q, "tensor").reshape(tokens, 2 * rank)
    e = dot(jnp.concatenate(split_high_low(warm), axis=0), error, 1, 1)
    e = e[:rank] + e[rank:]
    q, e = barrier((q, e))
    half_panel = shape((rank, feats // 2), F32)
    mine, other = call(part_kernel, (half_panel, half_panel), q, attn, e, flops=2 * 128 * feats * tokens, moved=MB)
    spread = call(spread_kernel, shape((zs, rank, feats // 2), BF16), mine, swap(other), moved=MB // 2)
    parts = exchange(spread, "dp", z_down)
    mine = call(functools.partial(mean_kernel, dp), half_panel, parts, moved=MB // 2)
    other = swap(mine)

    panel, packed = call(
        feature_kernel,
        (shape((rank, feats), F32), shape((group, rank, 2 * rank), BF16)),
        mine, other, attn, flops=4 * tokens * feats * rank, moved=2 * MB,
    )
    parts = exchange(packed, "tensor")
    rows = feats // 2
    error_term = call(
        error_term_kernel, shape((rank, width), F32), panel, error,
        grid=(feats // rows,),
        ins=[pl.BlockSpec((rank, rows), lambda i: (0, i)), pl.BlockSpec((rows, width), lambda i: (i, 0))],
        out_specs=pl.BlockSpec((rank, width), lambda i: (0, 0)),
        flops=4 * feats * width * rank, moved=6 * MB,
    )
    parts, error_term = barrier((parts, error_term))

    half_basis = shape((rank, half), F32)
    mine, other, gram = call(
        basis_term_kernel, (half_basis, shape((rank, half), BF16), shape((rank // 2, rank), F32)), parts, cot, error_term, moved=4 * MB
    )
    packed = call(pieces_kernel, shape((group, rank, half // group), BF16), mine, swap(other), moved=2 * MB)
    parts = exchange(packed, "tensor")
    inverse = call(inverse_kernel, shape((rank, rank), F32), gram, swap(gram), flops=5 * 10**9, moved=MB // 16)
    ortho = call(ortho_kernel, shape((feats, rank), BF16), panel, inverse, flops=10**8, moved=MB // 4)
    parts, inverse, ortho = barrier((parts, inverse, ortho))
    spread = call(sum_kernel, shape((zs, rank, half // group), BF16), parts, moved=MB // 2)
    parts = exchange(spread, "dp", z_up)
    grad_in = dot(cot_all, weight, 1, 1).astype(BF16)
    parts, grad_in = barrier((parts, grad_in))
    spread = call(
        functools.partial(basis_kernel, dp), shape((group, rank, half // group), BF16), parts, inverse, moved=MB // 2
    )
    mine = exchange(spread, "tensor")
    merged = (dot(attn, cot_all, 0, 0) + error.astype(F32)).astype(BF16)
    mine, merged = barrier((mine, merged))
    other = swap(mine)
    rows = feats // 2
    new_error, new_basis = call(
        final_kernel,
        (shape((feats, width), BF16), shape((rank, width), F32)),
        mine, other, ortho, merged,
        grid=(feats // rows,),
        ins=[anywhere] * 2
        + [pl.BlockSpec((rows, rank), lambda i: (i, 0)), pl.BlockSpec((rows, width), lambda i: (i, 0))],
        out_specs=(pl.BlockSpec((rows, width), lambda i: (i, 0)), pl.BlockSpec((rank, width), lambda i: (0, 0))),
        scratch=[
            pltpu.VMEM((rank, width), BF16),
            pltpu.VMEM(mine.shape, BF16),
            pltpu.VMEM(mine.shape, BF16),
            pltpu.SemaphoreType.DMA((2,)),
        ],
        flops=2 * feats * width * rank, moved=10 * MB, limit=60,
    )
    return grad_in, new_error, new_basis.T


def solution(mesh):
    in_specs = (
        P("dp", "tensor"),
        P(("dp", "tensor"), None),
        P("tensor", None),
        P(("dp", "tensor"), None),
        P(),
    )
    out_specs = (P("dp", "tensor"), P(("dp", "tensor"), None), P())
    return jax.shard_map(shards, mesh=mesh, in_specs=in_specs, out_specs=out_specs, check_vma=False)
```
